512 devices in a mesh: replica: 8 (over z_lo), fsdp: 64 (over z_hi, y, x, core).
Axes of the slice: x: 4, y: 4, z: 16 (z_hi: 2, z_lo: 8; z = z_hi * 8 + z_lo), core: 2. Of those that a mesh axis runs over, the one named last changes fastest.
Arguments:
- activations: bfloat16 [65536, 6144], P(('replica', 'fsdp')), may hold values from -400 to 400
- targets: bfloat16 [65536, 512], P(('replica', 'fsdp')), may hold values from -6 to 6
- weights: float32 [8, 6144, 512], P('replica', 'fsdp'), may hold values from -0.078125 to 0.078125
- first_moment: float32 [8, 6144, 512], P('replica', 'fsdp'), may hold values from -4 to 4
- second_moment: float32 [8, 6144, 512], P('replica', 'fsdp'), may hold values from 0.05 to 1
- local_frags: float32 [8, 2, 6144, 128], P('replica', None, 'fsdp'), may hold values from -6 to 6
- global_frags: float32 [2, 6144, 128], P(None, 'fsdp'), may hold values from -6 to 6
- momentum_frags: float32 [2, 6144, 128], P(None, 'fsdp'), may hold values from -6 to 6
- fragment_index: int32 [1], replicated, may hold values from 0 to 1
Outputs:
- new_weights: float32 [8, 6144, 512], P('replica', 'fsdp')
- new_first: float32 [8, 6144, 512], P('replica', 'fsdp')
- new_second: float32 [8, 6144, 512], P('replica', 'fsdp')
- new_global: float32 [6144, 128], P('fsdp')
- new_momentum: float32 [6144, 128], P('fsdp')
The draws below stay inside these ranges and needn't reach their ends.
All inputs are finite; a program needn't handle non-finite values.
Results may differ from the reference program's by a relative error of at most 0.0045.
Values may be sent and summed in bfloat16 or wider, within the bound.
No kernel may reach another device: no remote copies, remote signals or barrier semaphores. Data moves between devices by JAX's collectives and lax.ppermute only.
A program may use at most 64 MiB of HBM per device.

```python
import math
import jax
import jax.numpy as jnp
from jax import lax

D = 6144
KVW = 512
HD = 128
FRAGS = 2
REP_TOKENS = 8192
TOKENS = 65536
N_REPLICA = 8


def draw_activations(key, part):
    key = jax.random.fold_in(key, 11)
    key_rows, key_cols, key_base = jax.random.split(key, 3)
    row_scale = jnp.exp(jax.random.uniform(key_rows, (TOKENS, 1), jnp.float32, 0.0, math.log(10.0)))
    col_scale = jnp.exp(jax.random.uniform(key_cols, (1, D), jnp.float32, 0.0, math.log(10.0)))
    base = jnp.clip(jax.random.normal(key_base, (TOKENS, D), jnp.float32), -4.0, 4.0)
    return (base * row_scale * col_scale).astype(jnp.bfloat16)


def level_of(rng, extent, cuts, least, largest):
    level, own = 1.0, jax.random.fold_in(rng, 6)
    for position, blocks in cuts:
        draws = jnp.exp(jax.random.uniform(jax.random.fold_in(own, position), (blocks,), jnp.float32, least / len(cuts), largest / len(cuts)))
        level = level * jnp.repeat(draws, extent[position] // blocks).reshape([-1 if axis == position else 1 for axis in range(len(extent))])
    return level


def normal_values(rng, extent, scale, reach, cuts=(), dtype=jnp.bfloat16):
    factor_of = level_of(rng, extent, cuts, -0.22, 0.18) if cuts else 1.0
    values = jax.random.normal(rng, extent, jnp.float32) * scale * factor_of
    return jnp.minimum(jnp.maximum(values, -reach), reach).astype(dtype)


def setup_inputs(seed: int = 0) -> dict:
    streams_of = jax.random.split(jax.random.key(seed), 10)
    return {
        "activations": draw_activations(jax.random.fold_in(streams_of[9], 71), 0),
        "targets": normal_values(streams_of[1], (TOKENS, KVW), 1.0, 6.0, ((0, 512),)),
        "weights": normal_values(streams_of[2], (N_REPLICA, D, KVW), D ** -0.5, 0.078125, ((0, 8), (1, 64)), jnp.float32),
        "first_moment": normal_values(streams_of[3], (N_REPLICA, D, KVW), 0.3, 4.0, ((0, 8), (1, 64)), jnp.float32),
        "second_moment": jnp.clip(jnp.exp(math.log(1.0) - 2.9957323 * jax.random.uniform(streams_of[4], (N_REPLICA, D, KVW), jnp.float32) ** level_of(streams_of[4], (N_REPLICA, D, KVW), ((0, 8), (1, 64)), -0.2, 0.2)), 0.05, 1.0),
        "local_frags": normal_values(streams_of[5], (N_REPLICA, FRAGS, D, HD), 1.0, 6.0, ((0, 8), (2, 64)), jnp.float32),
        "global_frags": normal_values(streams_of[6], (FRAGS, D, HD), 1.0, 6.0, ((1, 64),), jnp.float32),
        "momentum_frags": normal_values(streams_of[7], (FRAGS, D, HD), 0.5, 6.0, ((1, 64),), jnp.float32),
        "fragment_index": jax.random.randint(streams_of[8], (1,), 0, FRAGS).astype(jnp.int32),
    }


def inner_step(items):
    tokens, goals, master, first, second = items
    wide = tokens.astype(jnp.float32)
    normed = (wide * lax.rsqrt(lax.optimization_barrier(jnp.mean(wide * wide, axis=1, keepdims=True)) + 1e-05)).astype(jnp.bfloat16)
    values = jnp.dot(normed, master.astype(jnp.bfloat16), preferred_element_type=jnp.float32)
    factor = float(REP_TOKENS) ** (-0.5)
    cotangent = ((values - goals.astype(jnp.float32)) * factor).astype(jnp.bfloat16)
    gradient = lax.dot_general(normed, cotangent, (((0,), (0,)), ((), ())), preferred_element_type=jnp.float32)
    new_first = 0.9 * first + 0.1 * gradient
    new_second = 0.95 * second + 0.05 * gradient * gradient
    new_master = master - 0.01 * (new_first / (jnp.sqrt(new_second) + 1e-08) + 0.1 * master)
    return (new_master, new_first, new_second)

def reference(activations, targets, weights, first_moment, second_moment, local_frags, global_frags, momentum_frags, fragment_index):
    tokens = activations.reshape(N_REPLICA, REP_TOKENS, D)
    goals = targets.reshape(N_REPLICA, REP_TOKENS, KVW)
    new_weights, new_first, new_second = lax.map(inner_step, (tokens, goals, weights, first_moment, second_moment))
    chosen = fragment_index[0]
    local_part = lax.dynamic_index_in_dim(local_frags, chosen, 1, False)
    global_part = lax.dynamic_index_in_dim(global_frags, chosen, 0, False)
    moment_part = lax.dynamic_index_in_dim(momentum_frags, chosen, 0, False)
    mean_delta = lax.optimization_barrier(jnp.sum(global_part[None] - local_part, axis=0)) / N_REPLICA
    new_momentum = 0.9 * moment_part + mean_delta
    new_global = global_part - 0.7 * (mean_delta + 0.9 * new_momentum)
    return (new_weights, new_first, new_second, new_global, new_momentum)
```

```python
import math

import jax
import jax.numpy as jnp
from jax import lax
from jax.sharding import Mesh
from jax.sharding import PartitionSpec as P

AXES = ("r", "z", "y", "x", "c")
FSDP = ("z", "y", "x", "c")


def swap(block, axes, distance):
    size = lax.axis_size(axes)
    return lax.ppermute(block, axes, [(i, i ^ distance) for i in range(size)])


def gather(block, axis):
    size = lax.axis_size(axis)
    return exchange(jnp.broadcast_to(block[None], (size, *block.shape)), axis)


def exchange(blocks, axes):
    return lax.all_to_all(blocks, axes, split_axis=0, concat_axis=0, tiled=True)


def on_device(
    activations,
    targets,
    weights,
    first_moment,
    second_moment,
    local_frags,
    global_frags,
    momentum_frags,
    fragment_index,
):
    f32, bf16 = jnp.float32, jnp.bfloat16
    nz, ny, nx, nc = (lax.axis_size(a) for a in FSDP)
    tokens, features = activations.shape
    rows, columns = weights.shape[1:]

    wide = activations.astype(f32)
    normed = (wide * lax.rsqrt(jnp.mean(wide * wide, axis=1, keepdims=True) + 1e-05)).astype(bf16)
    blocks = normed.T.reshape(nz, ny, nx, nc, rows, tokens).transpose(3, 2, 1, 0, 4, 5)
    blocks = blocks.reshape(nc * nx, ny * nz * rows, tokens)
    held = exchange(blocks, ("c", "x"))

    master = weights[0]
    low = gather(master.astype(bf16), "z")
    low = gather(low, "y").reshape(ny * nz * rows, columns)

    part = jnp.einsum("sft,fn->stn", held, low, preferred_element_type=f32)
    part = part.reshape(nc, nx, tokens, columns).astype(bf16)
    part = jnp.sum(exchange(part, "c").astype(f32), axis=0)
    part = jnp.sum(exchange(part.astype(bf16), "x").astype(f32), axis=0)

    factor = 1.0 / math.sqrt(tokens * nz * ny * nx * nc)
    cotangent = ((part - targets.astype(f32)) * factor).astype(bf16)
    every = gather(gather(cotangent, "x"), "c").reshape(nc * nx, tokens, columns)

    grad = jnp.einsum("sft,stn->fn", held, every, preferred_element_type=f32)
    grad = grad.reshape(ny, nz, rows, columns).astype(bf16)
    grad = jnp.sum(exchange(grad, "y").astype(f32), axis=0)
    gradient = jnp.sum(exchange(grad.astype(bf16), "z").astype(f32), axis=0)

    new_first = 0.9 * first_moment[0] + 0.1 * gradient
    new_second = 0.95 * second_moment[0] + 0.05 * gradient * gradient
    new_master = master - 0.01 * (new_first / (jnp.sqrt(new_second) + 1e-08) + 0.1 * master)

    chosen = fragment_index[0]
    local_part = lax.dynamic_index_in_dim(local_frags[0], chosen, 0, False)
    global_part = lax.dynamic_index_in_dim(global_frags, chosen, 0, False)
    moment_part = lax.dynamic_index_in_dim(momentum_frags, chosen, 0, False)
    delta = global_part - local_part
    replicas = lax.axis_size("r")
    distance = 1
    while distance < replicas:
        delta = delta + swap(delta, "r", distance)
        distance *= 2
    mean_delta = delta / replicas
    new_momentum = 0.9 * moment_part + mean_delta
    new_global = global_part - 0.7 * (mean_delta + 0.9 * new_momentum)
    return (new_master[None], new_first[None], new_second[None], new_global, new_momentum)


def solution(mesh):
    grid = Mesh(mesh.devices.reshape(mesh.shape["replica"], 2, 4, 4, 2), AXES)
    return jax.shard_map(
        on_device,
        mesh=grid,
        in_specs=(
            P(AXES, None),
            P(AXES, None),
            P("r", FSDP, None),
            P("r", FSDP, None),
            P("r", FSDP, None),
            P("r", None, FSDP, None),
            P(None, FSDP, None),
            P(None, FSDP, None),
            P(),
        ),
        out_specs=(
            P("r", FSDP, None),
            P("r", FSDP, None),
            P("r", FSDP, None),
            P(FSDP, None),
            P(FSDP, None),
        ),
        check_vma=False,
    )
```

```python
import functools
import math

import jax
import jax.numpy as jnp
from jax import lax
from jax.experimental import pallas as pl
from jax.experimental.pallas import tpu as pltpu
from jax.sharding import Mesh
from jax.sharding import PartitionSpec as P

AXES = ("r", "z", "y", "x", "c")
FSDP = ("z", "y", "x", "c")
VMEM = pl.BlockSpec(memory_space=pltpu.VMEM)


def swap(block, axis, distance=1):
    size = lax.axis_size(axis)
    return lax.ppermute(block, axis, [(i, i ^ distance) for i in range(size)])


def exchange(blocks, axes):
    return lax.all_to_all(blocks, axes, split_axis=0, concat_axis=0, tiled=True)


def spread(block, axis):
    size = lax.axis_size(axis)
    return exchange(jnp.broadcast_to(block[None], (size, *block.shape)), axis)


def norm_kernel(sizes, act_ref, out_ref, chunk_ref, block_ref, in_sems, out_sems):
    nz, ny, nxc, rows = sizes
    tokens, features = act_ref.shape
    width = nxc * rows
    parts = range(nz * ny)
    arrive = [
        pltpu.make_async_copy(act_ref.at[:, pl.ds(i * width, width)], chunk_ref.at[i], in_sems.at[i])
        for i in parts
    ]
    leave = [
        pltpu.make_async_copy(block_ref.at[i], out_ref.at[:, i % ny, i // ny], out_sems.at[i])
        for i in parts
    ]
    for copy in arrive:
        copy.start()
    total = jnp.zeros((tokens, 1), jnp.float32)
    for i in parts:
        arrive[i].wait()
        part = chunk_ref[i].astype(jnp.float32)
        total = total + jnp.sum(part * part, axis=1, keepdims=True)
    scale = lax.rsqrt(total * (1.0 / features) + 1e-05)
    for i in parts:
        part = (chunk_ref[i].astype(jnp.float32) * scale).astype(jnp.bfloat16)
        block_ref[i] = part.T.reshape(nxc, rows, tokens)
        leave[i].start()
    for copy in leave:
        copy.wait()


def normed_blocks(activations, sizes):
    nz, ny, nxc, rows = sizes
    tokens = activations.shape[0]
    return pl.pallas_call(
        functools.partial(norm_kernel, sizes),
        out_shape=jax.ShapeDtypeStruct((nxc, ny, nz, rows, tokens), jnp.bfloat16),
        in_specs=[pl.BlockSpec(memory_space=pltpu.HBM)],
        out_specs=pl.BlockSpec(memory_space=pltpu.HBM),
        scratch_shapes=[
            pltpu.VMEM((nz * ny, tokens, nxc * rows), jnp.bfloat16),
            pltpu.VMEM((nz * ny, nxc, rows, tokens), jnp.bfloat16),
            pltpu.SemaphoreType.DMA((nz * ny,)),
            pltpu.SemaphoreType.DMA((nz * ny,)),
        ],
        compiler_params=pltpu.CompilerParams(vmem_limit_bytes=60 * 2**20),
        cost_estimate=pl.CostEstimate(
            flops=8 * activations.size, bytes_accessed=4 * activations.size, transcendentals=0
        ),
    )(activations)


def on_device(
    activations,
    targets,
    weights,
    first_moment,
    second_moment,
    local_frags,
    global_frags,
    momentum_frags,
    fragment_index,
):
    f32, bf16 = jnp.float32, jnp.bfloat16
    nz, ny, nx, nc = (lax.axis_size(a) for a in FSDP)
    z, c = lax.axis_index("z"), lax.axis_index("c")
    tokens, features = act_ref.shape
    width = nxc * rows
    parts = range(nz * ny)
    arrive = [
        pltpu.make_async_copy(act_ref.at[:, pl.ds(i * width, width)], chunk_ref.at[i], in_sems.at[i])
        for i in parts
    ]
    leave = [
        pltpu.make_async_copy(block_ref.at[i], out_ref.at[:, i % ny, i // ny], out_sems.at[i])
        for i in parts
    ]
    for copy in arrive:
        copy.start()
    total = jnp.zeros((tokens, 1), jnp.float32)
    for i in parts:
        arrive[i].wait()
        part = chunk_ref[i].astype(jnp.float32)
        total = total + jnp.sum(part * part, axis=1, keepdims=True)
    scale = lax.rsqrt(total * (1.0 / features) + 1e-05)
    for i in parts:
        part = (chunk_ref[i].astype(jnp.float32) * scale).astype(jnp.bfloat16)
        block_ref[i] = part.T.reshape(nxc, rows, tokens)
        leave[i].start()
    for copy in leave:
        copy.wait()


def normed_blocks(activations, sizes):
    nz, ny, nxc, rows = sizes
    tokens = activations.shape[0]
    return pl.pallas_call(
        functools.partial(norm_kernel, sizes),
        out_shape=jax.ShapeDtypeStruct((nxc, ny, nz, rows, tokens), jnp.bfloat16),
        in_specs=[pl.BlockSpec(memory_space=pltpu.HBM)],
        out_specs=pl.BlockSpec(memory_space=pltpu.HBM),
        scratch_shapes=[
            pltpu.VMEM((nz * ny, tokens, nxc * rows), jnp.bfloat16),
            pltpu.VMEM((nz * ny, nxc, rows, tokens), jnp.bfloat16),
            pltpu.SemaphoreType.DMA((nz * ny,)),
            pltpu.SemaphoreType.DMA((nz * ny,)),
        ],
        compiler_params=pltpu.CompilerParams(vmem_limit_bytes=60 * 2**20),
        cost_estimate=pl.CostEstimate(
            flops=8 * activations.size, bytes_accessed=4 * activations.size, transcendentals=0
        ),
    )(activations)


def on_device(
    activations,
    targets,
    weights,
    first_moment,
    second_moment,
    local_frags,
    global_frags,
    momentum_frags,
    fragment_index,
):
    f32, bf16 = jnp.float32, jnp.bfloat16
    nz, ny, nx, nc = (lax.axis_size(a) for a in FSDP)
    z, y, x, c = (lax.axis_index(a) for a in FSDP)
    tokens, features = activations.shape
    rows, columns = weights.shape[1:]
    group = ny * nz * rows

    chosen = fragment_index[0]
    local_part = lax.dynamic_index_in_dim(local_frags[0], chosen, 0, False)
    global_part = lax.dynamic_index_in_dim(global_frags, chosen, 0, False)
    moment_part = lax.dynamic_index_in_dim(momentum_frags, chosen, 0, False)
    delta = global_part - local_part

    master = weights[0]
    low = lax.all_gather(master.astype(bf16), "z")
    low = lax.all_gather(low, "y").reshape(group, columns)

    blocks = normed_blocks(activations, (nz, ny, nx * nc, rows))
    held = exchange(blocks.reshape(nx * nc, group, tokens), ("x", "c"))

    held = held.reshape(nx, nc, group, tokens)
    mine = lax.dynamic_index_in_dim(held, c, 1, False)
    theirs = lax.dynamic_index_in_dim(held, 1 - c, 1, False)

    send = jnp.einsum("sft,fn->stn", theirs, low, preferred_element_type=f32).astype(bf16)
    part = jnp.einsum("sft,fn->stn", mine, low, preferred_element_type=f32)
    part = lax.optimization_barrier(part) + swap(send, "c").astype(f32)
    part, delta = lax.optimization_barrier((part.astype(bf16), delta))
    arrived = swap(delta, "r", 1)
    part, arrived = lax.optimization_barrier((exchange(part, "x"), arrived))
    delta = delta + arrived
    part = part.astype(f32)
    factor = 1.0 / math.sqrt(tokens * nz * ny * nx * nc)
    cotangent = ((jnp.sum(part, axis=0) - targets.astype(f32)) * factor).astype(bf16)
    cotangent, delta = lax.optimization_barrier((cotangent, delta))
    arrived = swap(delta, "r", 2)
    near = spread(cotangent, "x")
    near, arrived = lax.optimization_barrier((near, arrived))
    delta = delta + arrived
    far = swap(near, "c")

    grad = jnp.einsum("sft,stn->fn", mine, near, preferred_element_type=f32)
    grad = grad + jnp.einsum("sft,stn->fn", theirs, far, preferred_element_type=f32)
    grad = grad.reshape(ny, nz, rows, columns).astype(bf16)
    delta, grad = lax.optimization_barrier((delta, grad))
    arrived = swap(delta, "r", 4)
    grad = exchange(grad, "y")
    grad, arrived = lax.optimization_barrier((grad, arrived))
    delta = delta + arrived
    grad = jnp.sum(grad.astype(f32), axis=0)
    sent = lax.dynamic_index_in_dim(grad, 1 - z, 0, False).astype(bf16)
    kept = lax.dynamic_index_in_dim(grad, z, 0, False)
    gradient = kept + swap(sent, "z").astype(f32)

    new_first = 0.9 * first_moment[0] + 0.1 * gradient
    new_second = 0.95 * second_moment[0] + 0.05 * gradient * gradient
    new_master = master - 0.01 * (new_first / (jnp.sqrt(new_second) + 1e-08) + 0.1 * master)

    mean_delta = delta / lax.axis_size("r")
    new_momentum = 0.9 * moment_part + mean_delta
    new_global = global_part - 0.7 * (mean_delta + 0.9 * new_momentum)
    return (new_master[None], new_first[None], new_second[None], new_global, new_momentum)


def solution(mesh):
    grid = Mesh(mesh.devices.reshape(mesh.shape["replica"], 2, 4, 4, 2), AXES)
    return jax.shard_map(
        on_device,
        mesh=grid,
        in_specs=(
            P(AXES, None),
            P(AXES, None),
            P("r", FSDP, None),
            P("r", FSDP, None),
            P("r", FSDP, None),
            P("r", None, FSDP, None),
            P(None, FSDP, None),
            P(None, FSDP, None),
            P(),
        ),
        out_specs=(
            P("r", FSDP, None),
            P("r", FSDP, None),
            P("r", FSDP, None),
            P(FSDP, None),
            P(FSDP, None),
        ),
        check_vma=False,
    )
```

```python
import functools
import math

import jax
import jax.numpy as jnp
from jax import lax
from jax.experimental import pallas as pl
from jax.experimental.pallas import tpu as pltpu
from jax.sharding import Mesh
from jax.sharding import PartitionSpec as P

AXES = ("r", "z", "y", "x", "c")
FSDP = ("z", "y", "x", "c")
VMEM = pl.BlockSpec(memory_space=pltpu.VMEM)


def swap(block, axis, distance=1):
    size = lax.axis_size(axis)
    return lax.ppermute(block, axis, [(i, i ^ distance) for i in range(size)])


def exchange(blocks, axes):
    return lax.all_to_all(blocks, axes, split_axis=0, concat_axis=0, tiled=True)


def spread(block, axis):
    size = lax.axis_size(axis)
    return exchange(jnp.broadcast_to(block[None], (size, *block.shape)), axis)


def norm_kernel(sizes, act_ref, out_ref, chunk_ref, block_ref, in_sems, out_sems):
    nz, ny, nxc, rows = sizes
    tokens, features = act_ref.shape
    width, lanes, step = nxc * rows, 128, 256
    parts = range(nz * ny)
    arrive = [
        pltpu.make_async_copy(act_ref.at[:, pl.ds(i * width, width)], chunk_ref.at[i], in_sems.at[i])
        for i in parts
    ]
    leave = [
        pltpu.make_async_copy(block_ref.at[i], out_ref.at[:, i % ny, i // ny], out_sems.at[i])
        for i in parts
    ]
    for copy in arrive:
        copy.start()
    total = jnp.zeros((tokens, lanes), jnp.float32)
    for i in parts:
        arrive[i].wait()
        for k in range(0, width, lanes):
            part = chunk_ref[i, :, k : k + lanes].astype(jnp.float32)
            total = total + part * part
    total = jnp.sum(total, axis=1, keepdims=True)
    scale = lax.rsqrt(total * (1.0 / features) + 1e-05)
    scale = jnp.broadcast_to(scale, (tokens, lanes)).T[:1]
    one = (
        lax.broadcasted_iota(jnp.int32, (step, step), 0) == lax.broadcasted_iota(jnp.int32, (step, step), 1)
    ).astype(jnp.bfloat16)
    for i in parts:
        turned = [
            lax.dot_general(
                one,
                chunk_ref[i, :, k : k + step],
                (((1,), (1,)), ((), ())),
                preferred_element_type=jnp.float32,
            )
            for k in range(0, width, step)
        ]
        turned = (jnp.concatenate(turned, axis=0) * scale).astype(jnp.bfloat16)
        block_ref[i] = turned.reshape(nxc, rows, tokens)
        leave[i].start()
    for copy in leave:
        copy.wait()


def normed_blocks(activations, sizes):
    nz, ny, nxc, rows = sizes
    tokens = activations.shape[0]
    return pl.pallas_call(
        functools.partial(norm_kernel, sizes),
        out_shape=jax.ShapeDtypeStruct((nxc, ny, nz, rows, tokens), jnp.bfloat16),
        in_specs=[pl.BlockSpec(memory_space=pltpu.HBM)],
        out_specs=pl.BlockSpec(memory_space=pltpu.HBM),
        scratch_shapes=[
            pltpu.VMEM((nz * ny, tokens, nxc * rows), jnp.bfloat16),
            pltpu.VMEM((nz * ny, nxc, rows, tokens), jnp.bfloat16),
            pltpu.SemaphoreType.DMA((nz * ny,)),
            pltpu.SemaphoreType.DMA((nz * ny,)),
        ],
        compiler_params=pltpu.CompilerParams(vmem_limit_bytes=60 * 2**20),
        cost_estimate=pl.CostEstimate(
            flops=8 * activations.size, bytes_accessed=4 * activations.size, transcendentals=0
        ),
    )(activations)


def add_kernel(kept_ref, came_ref, out_ref, block_ref, sems):
    leave = [pltpu.make_async_copy(block_ref.at[i], out_ref.at[i], sems.at[i]) for i in range(out_ref.shape[0])]
    for i, copy in enumerate(leave):
        block_ref[i] = (kept_ref[i] + came_ref[i].astype(jnp.float32)).astype(block_ref.dtype)
        copy.start()
    for copy in leave:
        copy.wait()


def add_blocks(kept, came):
    return pl.pallas_call(
        add_kernel,
        out_shape=jax.ShapeDtypeStruct(came.shape, came.dtype),
        in_specs=[VMEM, VMEM],
        out_specs=pl.BlockSpec(memory_space=pltpu.HBM),
        scratch_shapes=[pltpu.VMEM(came.shape, came.dtype), pltpu.SemaphoreType.DMA((came.shape[0],))],
        compiler_params=pltpu.CompilerParams(vmem_limit_bytes=16 * 2**20),
        cost_estimate=pl.CostEstimate(flops=came.size, bytes_accessed=8 * came.size, transcendentals=0),
    )(kept, came)


def on_device(
    activations,
    targets,
    weights,
    first_moment,
    second_moment,
    local_frags,
    global_frags,
    momentum_frags,
    fragment_index,
):
    f32, bf16 = jnp.float32, jnp.bfloat16
    nz, ny, nx, nc = (lax.axis_size(a) for a in FSDP)
    z, c = lax.axis_index("z"), lax.axis_index("c")
    tokens, features = act_ref.shape
    width = nxc * rows
    parts = range(nz * ny)
    arrive = [
        pltpu.make_async_copy(act_ref.at[:, pl.ds(i * width, width)], chunk_ref.at[i], in_sems.at[i])
        for i in parts
    ]
    leave = [
        pltpu.make_async_copy(block_ref.at[i], out_ref.at[:, i % ny, i // ny], out_sems.at[i])
        for i in parts
    ]
    for copy in arrive:
        copy.start()
    total = jnp.zeros((tokens, 1), jnp.float32)
    for i in parts:
        arrive[i].wait()
        part = chunk_ref[i].astype(jnp.float32)
        total = total + jnp.sum(part * part, axis=1, keepdims=True)
    scale = lax.rsqrt(total * (1.0 / features) + 1e-05)
    for i in parts:
        part = (chunk_ref[i].astype(jnp.float32) * scale).astype(jnp.bfloat16)
        block_ref[i] = part.T.reshape(nxc, rows, tokens)
        leave[i].start()
    for copy in leave:
        copy.wait()


def normed_blocks(activations, sizes):
    nz, ny, nxc, rows = sizes
    tokens = activations.shape[0]
    return pl.pallas_call(
        functools.partial(norm_kernel, sizes),
        out_shape=jax.ShapeDtypeStruct((nxc, ny, nz, rows, tokens), jnp.bfloat16),
        in_specs=[pl.BlockSpec(memory_space=pltpu.HBM)],
        out_specs=pl.BlockSpec(memory_space=pltpu.HBM),
        scratch_shapes=[
            pltpu.VMEM((nz * ny, tokens, nxc * rows), jnp.bfloat16),
            pltpu.VMEM((nz * ny, nxc, rows, tokens), jnp.bfloat16),
            pltpu.SemaphoreType.DMA((nz * ny,)),
            pltpu.SemaphoreType.DMA((nz * ny,)),
        ],
        compiler_params=pltpu.CompilerParams(vmem_limit_bytes=60 * 2**20),
        cost_estimate=pl.CostEstimate(
            flops=8 * activations.size, bytes_accessed=4 * activations.size, transcendentals=0
        ),
    )(activations)


def on_device(
    activations,
    targets,
    weights,
    first_moment,
    second_moment,
    local_frags,
    global_frags,
    momentum_frags,
    fragment_index,
):
    f32, bf16 = jnp.float32, jnp.bfloat16
    nz, ny, nx, nc = (lax.axis_size(a) for a in FSDP)
    z, y, x, c = (lax.axis_index(a) for a in FSDP)
    tokens, features = activations.shape
    rows, columns = weights.shape[1:]
    group = ny * nz * rows

    chosen = fragment_index[0]
    local_part = lax.dynamic_index_in_dim(local_frags[0], chosen, 0, False)
    global_part = lax.dynamic_index_in_dim(global_frags, chosen, 0, False)
    moment_part = lax.dynamic_index_in_dim(momentum_frags, chosen, 0, False)
    delta = global_part - local_part

    master = weights[0]
    low = lax.all_gather(master.astype(bf16), "z")
    low = lax.all_gather(low, "y").reshape(group, columns)

    blocks = normed_blocks(activations, (nz, ny, nx * nc, rows))
    held = exchange(blocks.reshape(nx * nc, group, tokens), ("x", "c"))

    held = held.reshape(nx, nc, group, tokens)
    mine = lax.dynamic_index_in_dim(held, c, 1, False)
    theirs = lax.dynamic_index_in_dim(held, 1 - c, 1, False)

    send = jnp.einsum("sft,fn->stn", theirs, low, preferred_element_type=f32).astype(bf16)
    part = jnp.einsum("sft,fn->stn", mine, low, preferred_element_type=f32)
    part = add_blocks(part, swap(send, "c"))
    part, delta = lax.optimization_barrier((part, delta))
    arrived = swap(delta, "r", 1)
    part, arrived = lax.optimization_barrier((exchange(part, "x"), arrived))
    delta = delta + arrived
    part = part.astype(f32)
    factor = 1.0 / math.sqrt(tokens * nz * ny * nx * nc)
    cotangent = ((jnp.sum(part, axis=0) - targets.astype(f32)) * factor).astype(bf16)
    cotangent, delta = lax.optimization_barrier((cotangent, delta))
    arrived = swap(delta, "r", 2)
    near = spread(cotangent, "x")
    near, arrived = lax.optimization_barrier((near, arrived))
    delta = delta + arrived
    far = swap(near, "c")

    grad = jnp.einsum("sft,stn->fn", mine, near, preferred_element_type=f32)
    grad = grad + jnp.einsum("sft,stn->fn", theirs, far, preferred_element_type=f32)
    grad = grad.reshape(ny, nz, rows, columns).astype(bf16)
    delta, grad = lax.optimization_barrier((delta, grad))
    arrived = swap(delta, "r", 4)
    grad = exchange(grad, "y")
    grad, arrived = lax.optimization_barrier((grad, arrived))
    delta = delta + arrived
    grad = jnp.sum(grad.astype(f32), axis=0)
    sent = lax.dynamic_index_in_dim(grad, 1 - z, 0, False).astype(bf16)
    kept = lax.dynamic_index_in_dim(grad, z, 0, False)
    came = lax.dynamic_index_in_dim(lax.all_gather(sent, "z"), 1 - z, 0, False)
    gradient = kept + came.astype(f32)

    new_first = 0.9 * first_moment[0] + 0.1 * gradient
    new_second = 0.95 * second_moment[0] + 0.05 * gradient * gradient
    new_master = master - 0.01 * (new_first / (jnp.sqrt(new_second) + 1e-08) + 0.1 * master)

    mean_delta = delta / lax.axis_size("r")
    new_momentum = 0.9 * moment_part + mean_delta
    new_global = global_part - 0.7 * (mean_delta + 0.9 * new_momentum)
    return (new_master[None], new_first[None], new_second[None], new_global, new_momentum)


def solution(mesh):
    grid = Mesh(mesh.devices.reshape(mesh.shape["replica"], 2, 4, 4, 2), AXES)
    return jax.shard_map(
        on_device,
        mesh=grid,
        in_specs=(
            P(AXES, None),
            P(AXES, None),
            P("r", FSDP, None),
            P("r", FSDP, None),
            P("r", FSDP, None),
            P("r", None, FSDP, None),
            P(None, FSDP, None),
            P(None, FSDP, None),
            P(),
        ),
        out_specs=(
            P("r", FSDP, None),
            P("r", FSDP, None),
            P("r", FSDP, None),
            P(FSDP, None),
            P(FSDP, None),
        ),
        check_vma=False,
    )
```

```python
import functools
import math

import jax
import jax.numpy as jnp
from jax import lax
from jax.experimental import pallas as pl
from jax.experimental.pallas import tpu as pltpu
from jax.sharding import Mesh
from jax.sharding import PartitionSpec as P

AXES = ("r", "z", "y", "x", "c")
FSDP = ("z", "y", "x", "c")
VMEM = pl.BlockSpec(memory_space=pltpu.VMEM)


def swap(block, axis, distance=1):
    size = lax.axis_size(axis)
    return lax.ppermute(block, axis, [(i, i ^ distance) for i in range(size)])


def exchange(blocks, axes):
    return lax.all_to_all(blocks, axes, split_axis=0, concat_axis=0, tiled=True)


def spread(block, axis):
    size = lax.axis_size(axis)
    return exchange(jnp.broadcast_to(block[None], (size, *block.shape)), axis)


def norm_kernel(sizes, act_ref, out_ref, chunk_ref, block_ref, in_sems, out_sems):
    nz, ny, nxc, rows = sizes
    tokens, features = act_ref.shape
    width, lanes, step = nxc * rows, 128, 256
    parts = range(nz * ny)
    arrive = [
        pltpu.make_async_copy(act_ref.at[:, pl.ds(i * width, width)], chunk_ref.at[i], in_sems.at[i])
        for i in parts
    ]
    leave = [
        pltpu.make_async_copy(block_ref.at[i], out_ref.at[:, i % ny, i // ny], out_sems.at[i])
        for i in parts
    ]
    for copy in arrive:
        copy.start()
    total = jnp.zeros((tokens, lanes), jnp.float32)
    for i in parts:
        arrive[i].wait()
        for k in range(0, width, lanes):
            part = chunk_ref[i, :, k : k + lanes].astype(jnp.float32)
            total = total + part * part
    total = jnp.sum(total, axis=1, keepdims=True)
    scale = lax.rsqrt(total * (1.0 / features) + 1e-05)
    scale = jnp.broadcast_to(scale, (tokens, lanes)).T[:1]
    one = (
        lax.broadcasted_iota(jnp.int32, (step, step), 0) == lax.broadcasted_iota(jnp.int32, (step, step), 1)
    ).astype(jnp.bfloat16)
    for i in parts:
        turned = [
            lax.dot_general(
                one,
                chunk_ref[i, :, k : k + step],
                (((1,), (1,)), ((), ())),
                preferred_element_type=jnp.float32,
            )
            for k in range(0, width, step)
        ]
        turned = (jnp.concatenate(turned, axis=0) * scale).astype(jnp.bfloat16)
        block_ref[i] = turned.reshape(nxc, rows, tokens)
        leave[i].start()
    for copy in leave:
        copy.wait()


def normed_blocks(activations, sizes):
    nz, ny, nxc, rows = sizes
    tokens = activations.shape[0]
    return pl.pallas_call(
        functools.partial(norm_kernel, sizes),
        out_shape=jax.ShapeDtypeStruct((nxc, ny, nz, rows, tokens), jnp.bfloat16),
        in_specs=[pl.BlockSpec(memory_space=pltpu.HBM)],
        out_specs=pl.BlockSpec(memory_space=pltpu.HBM),
        scratch_shapes=[
            pltpu.VMEM((nz * ny, tokens, nxc * rows), jnp.bfloat16),
            pltpu.VMEM((nz * ny, nxc, rows, tokens), jnp.bfloat16),
            pltpu.SemaphoreType.DMA((nz * ny,)),
            pltpu.SemaphoreType.DMA((nz * ny,)),
        ],
        compiler_params=pltpu.CompilerParams(vmem_limit_bytes=60 * 2**20),
        cost_estimate=pl.CostEstimate(
            flops=8 * activations.size, bytes_accessed=4 * activations.size, transcendentals=0
        ),
    )(activations)


def add_kernel(kept_ref, came_ref, out_ref, block_ref, sems):
    leave = [pltpu.make_async_copy(block_ref.at[i], out_ref.at[i], sems.at[i]) for i in range(out_ref.shape[0])]
    for i, copy in enumerate(leave):
        block_ref[i] = (kept_ref[i] + came_ref[i].astype(jnp.float32)).astype(block_ref.dtype)
        copy.start()
    for copy in leave:
        copy.wait()


def add_blocks(kept, came):
    return pl.pallas_call(
        add_kernel,
        out_shape=jax.ShapeDtypeStruct(came.shape, came.dtype),
        in_specs=[VMEM, VMEM],
        out_specs=pl.BlockSpec(memory_space=pltpu.HBM),
        scratch_shapes=[pltpu.VMEM(came.shape, came.dtype), pltpu.SemaphoreType.DMA((came.shape[0],))],
        compiler_params=pltpu.CompilerParams(vmem_limit_bytes=16 * 2**20),
        cost_estimate=pl.CostEstimate(flops=came.size, bytes_accessed=8 * came.size, transcendentals=0),
    )(kept, came)


def on_device(
    activations,
    targets,
    weights,
    first_moment,
    second_moment,
    local_frags,
    global_frags,
    momentum_frags,
    fragment_index,
):
    f32, bf16 = jnp.float32, jnp.bfloat16
    nz, ny, nx, nc = (lax.axis_size(a) for a in FSDP)
    z, c = lax.axis_index("z"), lax.axis_index("c")
    tokens, features = act_ref.shape
    width = nxc * rows
    parts = range(nz * ny)
    arrive = [
        pltpu.make_async_copy(act_ref.at[:, pl.ds(i * width, width)], chunk_ref.at[i], in_sems.at[i])
        for i in parts
    ]
    leave = [
        pltpu.make_async_copy(block_ref.at[i], out_ref.at[:, i % ny, i // ny], out_sems.at[i])
        for i in parts
    ]
    for copy in arrive:
        copy.start()
    total = jnp.zeros((tokens, 1), jnp.float32)
    for i in parts:
        arrive[i].wait()
        part = chunk_ref[i].astype(jnp.float32)
        total = total + jnp.sum(part * part, axis=1, keepdims=True)
    scale = lax.rsqrt(total * (1.0 / features) + 1e-05)
    for i in parts:
        part = (chunk_ref[i].astype(jnp.float32) * scale).astype(jnp.bfloat16)
        block_ref[i] = part.T.reshape(nxc, rows, tokens)
        leave[i].start()
    for copy in leave:
        copy.wait()


def normed_blocks(activations, sizes):
    nz, ny, nxc, rows = sizes
    tokens = activations.shape[0]
    return pl.pallas_call(
        functools.partial(norm_kernel, sizes),
        out_shape=jax.ShapeDtypeStruct((nxc, ny, nz, rows, tokens), jnp.bfloat16),
        in_specs=[pl.BlockSpec(memory_space=pltpu.HBM)],
        out_specs=pl.BlockSpec(memory_space=pltpu.HBM),
        scratch_shapes=[
            pltpu.VMEM((nz * ny, tokens, nxc * rows), jnp.bfloat16),
            pltpu.VMEM((nz * ny, nxc, rows, tokens), jnp.bfloat16),
            pltpu.SemaphoreType.DMA((nz * ny,)),
            pltpu.SemaphoreType.DMA((nz * ny,)),
        ],
        compiler_params=pltpu.CompilerParams(vmem_limit_bytes=60 * 2**20),
        cost_estimate=pl.CostEstimate(
            flops=8 * activations.size, bytes_accessed=4 * activations.size, transcendentals=0
        ),
    )(activations)


def on_device(
    activations,
    targets,
    weights,
    first_moment,
    second_moment,
    local_frags,
    global_frags,
    momentum_frags,
    fragment_index,
):
    f32, bf16 = jnp.float32, jnp.bfloat16
    nz, ny, nx, nc = (lax.axis_size(a) for a in FSDP)
    z, y, x, c = (lax.axis_index(a) for a in FSDP)
    tokens, features = activations.shape
    rows, columns = weights.shape[1:]
    group = ny * nz * rows

    chosen = fragment_index[0]
    local_part = lax.dynamic_index_in_dim(local_frags[0], chosen, 0, False)
    global_part = lax.dynamic_index_in_dim(global_frags, chosen, 0, False)
    moment_part = lax.dynamic_index_in_dim(momentum_frags, chosen, 0, False)
    delta = global_part - local_part

    master = weights[0]
    low = lax.all_gather(master.astype(bf16), "z")
    low = lax.all_gather(low, "y").reshape(group, columns)

    blocks = normed_blocks(activations, (nz, ny, nx * nc, rows))
    held = exchange(blocks.reshape(nx * nc, group, tokens), ("x", "c"))

    held = held.reshape(nx, nc, group, tokens)
    mine = lax.dynamic_index_in_dim(held, c, 1, False)
    theirs = lax.dynamic_index_in_dim(held, 1 - c, 1, False)

    send = jnp.einsum("sft,fn->stn", theirs, low, preferred_element_type=f32).astype(bf16)
    part = jnp.einsum("sft,fn->stn", mine, low, preferred_element_type=f32)
    part = add_blocks(part, swap(send, "c"))
    part, delta = lax.optimization_barrier((part, delta))
    arrived = swap(delta, "r", 1)
    part, arrived = lax.optimization_barrier((exchange(part, "x"), arrived))
    delta = delta + arrived
    part = part.astype(f32)
    factor = 1.0 / math.sqrt(tokens * nz * ny * nx * nc)
    cotangent = ((jnp.sum(part, axis=0) - targets.astype(f32)) * factor).astype(bf16)
    cotangent, delta = lax.optimization_barrier((cotangent, delta))
    arrived = swap(delta, "r", 2)
    near = spread(cotangent, "x")
    near, arrived = lax.optimization_barrier((near, arrived))
    delta = delta + arrived
    far = swap(near, "c")

    grad = jnp.einsum("sft,stn->fn", mine, near, preferred_element_type=f32)
    grad = grad + jnp.einsum("sft,stn->fn", theirs, far, preferred_element_type=f32)
    grad = grad.reshape(ny, nz, rows, columns).astype(bf16)
    delta, grad = lax.optimization_barrier((delta, grad))
    arrived = swap(delta, "r", 4)
    grad = exchange(grad, "y")
    mean_delta = (delta + arrived) / lax.axis_size("r")
    new_momentum = 0.9 * moment_part + mean_delta
    new_global = global_part - 0.7 * (mean_delta + 0.9 * new_momentum)
    grad, new_global, new_momentum = lax.optimization_barrier((grad, new_global, new_momentum))
    grad = jnp.sum(grad.astype(f32), axis=0)
    sent = lax.dynamic_index_in_dim(grad, 1 - z, 0, False).astype(bf16)
    kept = lax.dynamic_index_in_dim(grad, z, 0, False)
    came = lax.dynamic_index_in_dim(lax.all_gather(sent, "z"), 1 - z, 0, False)
    gradient = kept + came.astype(f32)

    new_first = 0.9 * first_moment[0] + 0.1 * gradient
    new_second = 0.95 * second_moment[0] + 0.05 * gradient * gradient
    new_master = master - 0.01 * (new_first / (jnp.sqrt(new_second) + 1e-08) + 0.1 * master)

    return (new_master[None], new_first[None], new_second[None], new_global, new_momentum)


def solution(mesh):
    grid = Mesh(mesh.devices.reshape(mesh.shape["replica"], 2, 4, 4, 2), AXES)
    return jax.shard_map(
        on_device,
        mesh=grid,
        in_specs=(
            P(AXES, None),
            P(AXES, None),
            P("r", FSDP, None),
            P("r", FSDP, None),
            P("r", FSDP, None),
            P("r", None, FSDP, None),
            P(None, FSDP, None),
            P(None, FSDP, None),
            P(),
        ),
        out_specs=(
            P("r", FSDP, None),
            P("r", FSDP, None),
            P("r", FSDP, None),
            P(FSDP, None),
            P(FSDP, None),
        ),
        check_vma=False,
    )
```

```python
import functools
import math

import jax
import jax.numpy as jnp
from jax import lax
from jax.experimental import pallas as pl
from jax.experimental.pallas import tpu as pltpu
from jax.sharding import Mesh
from jax.sharding import PartitionSpec as P

AXES = ("r", "z", "y", "x", "c")
FSDP = ("z", "y", "x", "c")
VMEM = pl.BlockSpec(memory_space=pltpu.VMEM)


def swap(block, axis, distance=1):
    size = lax.axis_size(axis)
    return lax.ppermute(block, axis, [(i, i ^ distance) for i in range(size)])


def pair_sum(block, axis, distance):
    groups = [[i, i ^ distance] for i in range(lax.axis_size(axis)) if not i & distance]
    both = lax.all_gather(block, axis, axis_index_groups=groups)
    return both[0] + both[1]


def exchange(blocks, axes):
    return lax.all_to_all(blocks, axes, split_axis=0, concat_axis=0, tiled=True)


def spread(block, axis):
    size = lax.axis_size(axis)
    return exchange(jnp.broadcast_to(block[None], (size, *block.shape)), axis)


def norm_kernel(sizes, act_ref, out_ref, chunk_ref, block_ref, in_sems, out_sems):
    nz, ny, nxc, rows = sizes
    tokens, features = act_ref.shape
    width, lanes, step = nxc * rows, 128, 256
    parts = range(nz * ny)
    arrive = [
        pltpu.make_async_copy(act_ref.at[:, pl.ds(i * width, width)], chunk_ref.at[i], in_sems.at[i])
        for i in parts
    ]
    leave = [
        pltpu.make_async_copy(block_ref.at[i], out_ref.at[:, i % ny, i // ny], out_sems.at[i])
        for i in parts
    ]
    for copy in arrive:
        copy.start()
    total = jnp.zeros((tokens, lanes), jnp.float32)
    for i in parts:
        arrive[i].wait()
        for k in range(0, width, lanes):
            part = chunk_ref[i, :, k : k + lanes].astype(jnp.float32)
            total = total + part * part
    total = jnp.sum(total, axis=1, keepdims=True)
    scale = lax.rsqrt(total * (1.0 / features) + 1e-05)
    scale = jnp.broadcast_to(scale, (tokens, lanes)).T[:1]
    one = (
        lax.broadcasted_iota(jnp.int32, (step, step), 0) == lax.broadcasted_iota(jnp.int32, (step, step), 1)
    ).astype(jnp.bfloat16)
    for i in parts:
        turned = [
            lax.dot_general(
                one,
                chunk_ref[i, :, k : k + step],
                (((1,), (1,)), ((), ())),
                preferred_element_type=jnp.float32,
            )
            for k in range(0, width, step)
        ]
        turned = (jnp.concatenate(turned, axis=0) * scale).astype(jnp.bfloat16)
        block_ref[i] = turned.reshape(nxc, rows, tokens)
        leave[i].start()
    for copy in leave:
        copy.wait()


def normed_blocks(activations, sizes):
    nz, ny, nxc, rows = sizes
    tokens = activations.shape[0]
    return pl.pallas_call(
        functools.partial(norm_kernel, sizes),
        out_shape=jax.ShapeDtypeStruct((nxc, ny, nz, rows, tokens), jnp.bfloat16),
        in_specs=[pl.BlockSpec(memory_space=pltpu.HBM)],
        out_specs=pl.BlockSpec(memory_space=pltpu.HBM),
        scratch_shapes=[
            pltpu.VMEM((nz * ny, tokens, nxc * rows), jnp.bfloat16),
            pltpu.VMEM((nz * ny, nxc, rows, tokens), jnp.bfloat16),
            pltpu.SemaphoreType.DMA((nz * ny,)),
            pltpu.SemaphoreType.DMA((nz * ny,)),
        ],
        compiler_params=pltpu.CompilerParams(vmem_limit_bytes=60 * 2**20),
        cost_estimate=pl.CostEstimate(
            flops=8 * activations.size, bytes_accessed=4 * activations.size, transcendentals=0
        ),
    )(activations)


def add_kernel(kept_ref, came_ref, out_ref, block_ref, sems):
    leave = [pltpu.make_async_copy(block_ref.at[i], out_ref.at[i], sems.at[i]) for i in range(out_ref.shape[0])]
    for i, copy in enumerate(leave):
        block_ref[i] = (kept_ref[i] + came_ref[i].astype(jnp.float32)).astype(block_ref.dtype)
        copy.start()
    for copy in leave:
        copy.wait()


def add_blocks(kept, came):
    return pl.pallas_call(
        add_kernel,
        out_shape=jax.ShapeDtypeStruct(came.shape, came.dtype),
        in_specs=[VMEM, VMEM],
        out_specs=pl.BlockSpec(memory_space=pltpu.HBM),
        scratch_shapes=[pltpu.VMEM(came.shape, came.dtype), pltpu.SemaphoreType.DMA((came.shape[0],))],
        compiler_params=pltpu.CompilerParams(vmem_limit_bytes=16 * 2**20),
        cost_estimate=pl.CostEstimate(flops=came.size, bytes_accessed=8 * came.size, transcendentals=0),
    )(kept, came)


def cotangent_kernel(factor, part_ref, target_ref, out_ref):
    total = part_ref[0].astype(jnp.float32)
    for i in range(1, part_ref.shape[0]):
        total = total + part_ref[i].astype(jnp.float32)
    block = ((total - target_ref[...].astype(jnp.float32)) * factor).astype(out_ref.dtype)
    for i in range(out_ref.shape[0]):
        out_ref[i] = block


def cotangents(factor, part, target):
    return pl.pallas_call(
        functools.partial(cotangent_kernel, factor),
        out_shape=jax.ShapeDtypeStruct(part.shape, target.dtype),
        in_specs=[VMEM, VMEM],
        out_specs=VMEM,
        compiler_params=pltpu.CompilerParams(vmem_limit_bytes=8 * 2**20),
        cost_estimate=pl.CostEstimate(flops=2 * part.size, bytes_accessed=5 * part.size, transcendentals=0),
    )(part, target)


def on_device(
    activations,
    targets,
    weights,
    first_moment,
    second_moment,
    local_frags,
    global_frags,
    momentum_frags,
    fragment_index,
):
    f32, bf16 = jnp.float32, jnp.bfloat16
    nz, ny, nx, nc = (lax.axis_size(a) for a in FSDP)
    z, c = lax.axis_index("z"), lax.axis_index("c")
    tokens, features = act_ref.shape
    width = nxc * rows
    parts = range(nz * ny)
    arrive = [
        pltpu.make_async_copy(act_ref.at[:, pl.ds(i * width, width)], chunk_ref.at[i], in_sems.at[i])
        for i in parts
    ]
    leave = [
        pltpu.make_async_copy(block_ref.at[i], out_ref.at[:, i % ny, i // ny], out_sems.at[i])
        for i in parts
    ]
    for copy in arrive:
        copy.start()
    total = jnp.zeros((tokens, 1), jnp.float32)
    for i in parts:
        arrive[i].wait()
        part = chunk_ref[i].astype(jnp.float32)
        total = total + jnp.sum(part * part, axis=1, keepdims=True)
    scale = lax.rsqrt(total * (1.0 / features) + 1e-05)
    for i in parts:
        part = (chunk_ref[i].astype(jnp.float32) * scale).astype(jnp.bfloat16)
        block_ref[i] = part.T.reshape(nxc, rows, tokens)
        leave[i].start()
    for copy in leave:
        copy.wait()


def normed_blocks(activations, sizes):
    nz, ny, nxc, rows = sizes
    tokens = activations.shape[0]
    return pl.pallas_call(
        functools.partial(norm_kernel, sizes),
        out_shape=jax.ShapeDtypeStruct((nxc, ny, nz, rows, tokens), jnp.bfloat16),
        in_specs=[pl.BlockSpec(memory_space=pltpu.HBM)],
        out_specs=pl.BlockSpec(memory_space=pltpu.HBM),
        scratch_shapes=[
            pltpu.VMEM((nz * ny, tokens, nxc * rows), jnp.bfloat16),
            pltpu.VMEM((nz * ny, nxc, rows, tokens), jnp.bfloat16),
            pltpu.SemaphoreType.DMA((nz * ny,)),
            pltpu.SemaphoreType.DMA((nz * ny,)),
        ],
        compiler_params=pltpu.CompilerParams(vmem_limit_bytes=60 * 2**20),
        cost_estimate=pl.CostEstimate(
            flops=8 * activations.size, bytes_accessed=4 * activations.size, transcendentals=0
        ),
    )(activations)


def on_device(
    activations,
    targets,
    weights,
    first_moment,
    second_moment,
    local_frags,
    global_frags,
    momentum_frags,
    fragment_index,
):
    f32, bf16 = jnp.float32, jnp.bfloat16
    nz, ny, nx, nc = (lax.axis_size(a) for a in FSDP)
    z, y, x, c = (lax.axis_index(a) for a in FSDP)
    tokens, features = activations.shape
    rows, columns = weights.shape[1:]
    group = ny * nz * rows

    chosen = fragment_index[0]
    local_part = lax.dynamic_index_in_dim(local_frags[0], chosen, 0, False)
    global_part = lax.dynamic_index_in_dim(global_frags, chosen, 0, False)
    moment_part = lax.dynamic_index_in_dim(momentum_frags, chosen, 0, False)
    delta = global_part - local_part

    master = weights[0]
    low = lax.all_gather(master.astype(bf16), "z")
    low = lax.all_gather(low, "y").reshape(group, columns)

    blocks = normed_blocks(activations, (nz, ny, nx * nc, rows))
    held = exchange(blocks.reshape(nx * nc, group, tokens), ("x", "c"))

    held = held.reshape(nx, nc, group, tokens)
    mine = lax.dynamic_index_in_dim(held, c, 1, False)
    theirs = lax.dynamic_index_in_dim(held, 1 - c, 1, False)

    send = jnp.einsum("sft,fn->stn", theirs, low, preferred_element_type=f32).astype(bf16)
    part = jnp.einsum("sft,fn->stn", mine, low, preferred_element_type=f32)
    part = add_blocks(part, swap(send, "c"))
    part, delta = lax.optimization_barrier((part, delta))
    part, delta = lax.optimization_barrier((exchange(part, "x"), pair_sum(delta, "r", 1)))
    factor = 1.0 / math.sqrt(tokens * nz * ny * nx * nc)
    cotangent = cotangents(factor, part, targets)
    cotangent, delta = lax.optimization_barrier((cotangent, delta))
    near, delta = lax.optimization_barrier((exchange(cotangent, "x"), pair_sum(delta, "r", 2)))
    far = swap(near, "c")

    grad = jnp.einsum("sft,stn->fn", mine, near, preferred_element_type=f32)
    grad = grad + jnp.einsum("sft,stn->fn", theirs, far, preferred_element_type=f32)
    grad = grad.reshape(ny, nz, rows, columns).astype(bf16)
    delta, grad = lax.optimization_barrier((delta, grad))
    grad = exchange(grad, "y")
    mean_delta = pair_sum(delta, "r", 4) / lax.axis_size("r")
    new_momentum = 0.9 * moment_part + mean_delta
    new_global = global_part - 0.7 * (mean_delta + 0.9 * new_momentum)
    grad, new_global, new_momentum = lax.optimization_barrier((grad, new_global, new_momentum))
    grad = jnp.sum(grad.astype(f32), axis=0)
    sent = lax.dynamic_index_in_dim(grad, 1 - z, 0, False).astype(bf16)
    kept = lax.dynamic_index_in_dim(grad, z, 0, False)
    came = lax.dynamic_index_in_dim(lax.all_gather(sent, "z"), 1 - z, 0, False)
    gradient = kept + came.astype(f32)

    new_first = 0.9 * first_moment[0] + 0.1 * gradient
    new_second = 0.95 * second_moment[0] + 0.05 * gradient * gradient
    new_master = master - 0.01 * (new_first / (jnp.sqrt(new_second) + 1e-08) + 0.1 * master)

    return (new_master[None], new_first[None], new_second[None], new_global, new_momentum)


def solution(mesh):
    grid = Mesh(mesh.devices.reshape(mesh.shape["replica"], 2, 4, 4, 2), AXES)
    return jax.shard_map(
        on_device,
        mesh=grid,
        in_specs=(
            P(AXES, None),
            P(AXES, None),
            P("r", FSDP, None),
            P("r", FSDP, None),
            P("r", FSDP, None),
            P("r", None, FSDP, None),
            P(None, FSDP, None),
            P(None, FSDP, None),
            P(),
        ),
        out_specs=(
            P("r", FSDP, None),
            P("r", FSDP, None),
            P("r", FSDP, None),
            P(FSDP, None),
            P(FSDP, None),
        ),
        check_vma=False,
    )
```

```python
import functools
import math

import jax
import jax.numpy as jnp
from jax import lax
from jax.experimental import pallas as pl
from jax.experimental.pallas import tpu as pltpu
from jax.sharding import Mesh
from jax.sharding import PartitionSpec as P

AXES = ("r", "z", "y", "x", "c")
FSDP = ("z", "y", "x", "c")
VMEM = pl.BlockSpec(memory_space=pltpu.VMEM)


def swap(block, axis, distance=1):
    size = lax.axis_size(axis)
    return lax.ppermute(block, axis, [(i, i ^ distance) for i in range(size)])


def pair_sum(block, axis, distance):
    groups = [[i, i ^ distance] for i in range(lax.axis_size(axis)) if not i & distance]
    both = lax.all_gather(block, axis, axis_index_groups=groups)
    return both[0] + both[1]


def exchange(blocks, axes):
    return lax.all_to_all(blocks, axes, split_axis=0, concat_axis=0, tiled=True)


def spread(block, axis):
    size = lax.axis_size(axis)
    return exchange(jnp.broadcast_to(block[None], (size, *block.shape)), axis)


def norm_kernel(sizes, act_ref, out_ref, chunk_ref, block_ref, in_sems, out_sems):
    nz, ny, nxc, rows = sizes
    tokens, features = act_ref.shape
    width, lanes, step = nxc * rows, 128, 256
    parts = range(nz * ny)
    arrive = [
        pltpu.make_async_copy(act_ref.at[:, pl.ds(i * width, width)], chunk_ref.at[i], in_sems.at[i])
        for i in parts
    ]
    leave = [
        pltpu.make_async_copy(block_ref.at[i], out_ref.at[:, i % ny, i // ny], out_sems.at[i])
        for i in parts
    ]
    for copy in arrive:
        copy.start()
    total = jnp.zeros((tokens, lanes), jnp.float32)
    for i in parts:
        arrive[i].wait()
        for k in range(0, width, lanes):
            part = chunk_ref[i, :, k : k + lanes].astype(jnp.float32)
            total = total + part * part
    total = jnp.sum(total, axis=1, keepdims=True)
    scale = lax.rsqrt(total * (1.0 / features) + 1e-05)
    scale = jnp.broadcast_to(scale, (tokens, lanes)).T[:1]
    one = (
        lax.broadcasted_iota(jnp.int32, (step, step), 0) == lax.broadcasted_iota(jnp.int32, (step, step), 1)
    ).astype(jnp.bfloat16)
    for i in parts:
        turned = [
            lax.dot_general(
                one,
                chunk_ref[i, :, k : k + step],
                (((1,), (1,)), ((), ())),
                preferred_element_type=jnp.float32,
            )
            for k in range(0, width, step)
        ]
        turned = (jnp.concatenate(turned, axis=0) * scale).astype(jnp.bfloat16)
        block_ref[i] = turned.reshape(nxc, rows, tokens)
        leave[i].start()
    for copy in leave:
        copy.wait()


def normed_blocks(activations, sizes):
    nz, ny, nxc, rows = sizes
    tokens = activations.shape[0]
    return pl.pallas_call(
        functools.partial(norm_kernel, sizes),
        out_shape=jax.ShapeDtypeStruct((nxc, ny, nz, rows, tokens), jnp.bfloat16),
        in_specs=[pl.BlockSpec(memory_space=pltpu.HBM)],
        out_specs=pl.BlockSpec(memory_space=pltpu.HBM),
        scratch_shapes=[
            pltpu.VMEM((nz * ny, tokens, nxc * rows), jnp.bfloat16),
            pltpu.VMEM((nz * ny, nxc, rows, tokens), jnp.bfloat16),
            pltpu.SemaphoreType.DMA((nz * ny,)),
            pltpu.SemaphoreType.DMA((nz * ny,)),
        ],
        compiler_params=pltpu.CompilerParams(vmem_limit_bytes=60 * 2**20),
        cost_estimate=pl.CostEstimate(
            flops=8 * activations.size, bytes_accessed=4 * activations.size, transcendentals=0
        ),
    )(activations)


def add_kernel(kept_ref, came_ref, out_ref, block_ref, sems):
    leave = [pltpu.make_async_copy(block_ref.at[i], out_ref.at[i], sems.at[i]) for i in range(out_ref.shape[0])]
    for i, copy in enumerate(leave):
        block_ref[i] = (kept_ref[i] + came_ref[i].astype(jnp.float32)).astype(block_ref.dtype)
        copy.start()
    for copy in leave:
        copy.wait()


def add_blocks(kept, came):
    return pl.pallas_call(
        add_kernel,
        out_shape=jax.ShapeDtypeStruct(came.shape, came.dtype),
        in_specs=[VMEM, VMEM],
        out_specs=pl.BlockSpec(memory_space=pltpu.HBM),
        scratch_shapes=[pltpu.VMEM(came.shape, came.dtype), pltpu.SemaphoreType.DMA((came.shape[0],))],
        compiler_params=pltpu.CompilerParams(vmem_limit_bytes=16 * 2**20),
        cost_estimate=pl.CostEstimate(flops=came.size, bytes_accessed=8 * came.size, transcendentals=0),
    )(kept, came)


def cotangent_kernel(factor, part_ref, target_ref, out_ref):
    total = part_ref[0].astype(jnp.float32)
    for i in range(1, part_ref.shape[0]):
        total = total + part_ref[i].astype(jnp.float32)
    block = ((total - target_ref[...].astype(jnp.float32)) * factor).astype(out_ref.dtype)
    for i in range(out_ref.shape[0]):
        out_ref[i] = block


def cotangents(factor, part, target):
    return pl.pallas_call(
        functools.partial(cotangent_kernel, factor),
        out_shape=jax.ShapeDtypeStruct(part.shape, target.dtype),
        in_specs=[VMEM, VMEM],
        out_specs=VMEM,
        compiler_params=pltpu.CompilerParams(vmem_limit_bytes=8 * 2**20),
        cost_estimate=pl.CostEstimate(flops=2 * part.size, bytes_accessed=5 * part.size, transcendentals=0),
    )(part, target)


def on_device(
    activations,
    targets,
    weights,
    first_moment,
    second_moment,
    local_frags,
    global_frags,
    momentum_frags,
    fragment_index,
):
    f32, bf16 = jnp.float32, jnp.bfloat16
    nz, ny, nx, nc = (lax.axis_size(a) for a in FSDP)
    z, c = lax.axis_index("z"), lax.axis_index("c")
    tokens, features = act_ref.shape
    width = nxc * rows
    parts = range(nz * ny)
    arrive = [
        pltpu.make_async_copy(act_ref.at[:, pl.ds(i * width, width)], chunk_ref.at[i], in_sems.at[i])
        for i in parts
    ]
    leave = [
        pltpu.make_async_copy(block_ref.at[i], out_ref.at[:, i % ny, i // ny], out_sems.at[i])
        for i in parts
    ]
    for copy in arrive:
        copy.start()
    total = jnp.zeros((tokens, 1), jnp.float32)
    for i in parts:
        arrive[i].wait()
        part = chunk_ref[i].astype(jnp.float32)
        total = total + jnp.sum(part * part, axis=1, keepdims=True)
    scale = lax.rsqrt(total * (1.0 / features) + 1e-05)
    for i in parts:
        part = (chunk_ref[i].astype(jnp.float32) * scale).astype(jnp.bfloat16)
        block_ref[i] = part.T.reshape(nxc, rows, tokens)
        leave[i].start()
    for copy in leave:
        copy.wait()


def normed_blocks(activations, sizes):
    nz, ny, nxc, rows = sizes
    tokens = activations.shape[0]
    return pl.pallas_call(
        functools.partial(norm_kernel, sizes),
        out_shape=jax.ShapeDtypeStruct((nxc, ny, nz, rows, tokens), jnp.bfloat16),
        in_specs=[pl.BlockSpec(memory_space=pltpu.HBM)],
        out_specs=pl.BlockSpec(memory_space=pltpu.HBM),
        scratch_shapes=[
            pltpu.VMEM((nz * ny, tokens, nxc * rows), jnp.bfloat16),
            pltpu.VMEM((nz * ny, nxc, rows, tokens), jnp.bfloat16),
            pltpu.SemaphoreType.DMA((nz * ny,)),
            pltpu.SemaphoreType.DMA((nz * ny,)),
        ],
        compiler_params=pltpu.CompilerParams(vmem_limit_bytes=60 * 2**20),
        cost_estimate=pl.CostEstimate(
            flops=8 * activations.size, bytes_accessed=4 * activations.size, transcendentals=0
        ),
    )(activations)


def on_device(
    activations,
    targets,
    weights,
    first_moment,
    second_moment,
    local_frags,
    global_frags,
    momentum_frags,
    fragment_index,
):
    f32, bf16 = jnp.float32, jnp.bfloat16
    nz, ny, nx, nc = (lax.axis_size(a) for a in FSDP)
    z, y, x, c = (lax.axis_index(a) for a in FSDP)
    tokens, features = activations.shape
    rows, columns = weights.shape[1:]
    group = ny * nz * rows

    chosen = fragment_index[0]
    local_part = lax.dynamic_index_in_dim(local_frags[0], chosen, 0, False)
    global_part = lax.dynamic_index_in_dim(global_frags, chosen, 0, False)
    moment_part = lax.dynamic_index_in_dim(momentum_frags, chosen, 0, False)
    delta = global_part - local_part

    master = weights[0]
    low = lax.all_gather(master.astype(bf16), "z")
    low = lax.all_gather(low, "y").reshape(group, columns)

    blocks = normed_blocks(activations, (nz, ny, nx * nc, rows))
    held = exchange(blocks.reshape(nx * nc, group, tokens), ("x", "c"))

    held = held.reshape(nx, nc, group, tokens)
    mine = lax.dynamic_index_in_dim(held, c, 1, False)
    theirs = lax.dynamic_index_in_dim(held, 1 - c, 1, False)

    send = jnp.einsum("sft,fn->stn", theirs, low, preferred_element_type=f32).astype(bf16)
    part = jnp.einsum("sft,fn->stn", mine, low, preferred_element_type=f32)
    part = add_blocks(part, swap(send, "c"))
    part, delta = lax.optimization_barrier((exchange(part, "x"), pair_sum(delta, "r", 1)))
    factor = 1.0 / math.sqrt(tokens * nz * ny * nx * nc)
    cotangent = cotangents(factor, part, targets)
    cotangent, delta = lax.optimization_barrier((cotangent, delta))
    near, delta = lax.optimization_barrier((exchange(cotangent, "x"), pair_sum(delta, "r", 2)))
    far = swap(near, "c")

    grad = jnp.einsum("sft,stn->fn", mine, near, preferred_element_type=f32)
    grad = grad + jnp.einsum("sft,stn->fn", theirs, far, preferred_element_type=f32)
    grad = grad.reshape(ny, nz, rows, columns).astype(bf16)
    delta, grad = lax.optimization_barrier((delta, grad))
    grad = exchange(grad, "y")
    mean_delta = pair_sum(delta, "r", 4) / lax.axis_size("r")
    new_momentum = 0.9 * moment_part + mean_delta
    new_global = global_part - 0.7 * (mean_delta + 0.9 * new_momentum)
    grad, new_global, new_momentum = lax.optimization_barrier((grad, new_global, new_momentum))
    grad = jnp.sum(grad.astype(f32), axis=0)
    sent = lax.dynamic_index_in_dim(grad, 1 - z, 0, False).astype(bf16)
    kept = lax.dynamic_index_in_dim(grad, z, 0, False)
    came = lax.dynamic_index_in_dim(lax.all_gather(sent, "z"), 1 - z, 0, False)
    gradient = kept + came.astype(f32)

    new_first = 0.9 * first_moment[0] + 0.1 * gradient
    new_second = 0.95 * second_moment[0] + 0.05 * gradient * gradient
    new_master = master - 0.01 * (new_first / (jnp.sqrt(new_second) + 1e-08) + 0.1 * master)

    return (new_master[None], new_first[None], new_second[None], new_global, new_momentum)


def solution(mesh):
    grid = Mesh(mesh.devices.reshape(mesh.shape["replica"], 2, 4, 4, 2), AXES)
    return jax.shard_map(
        on_device,
        mesh=grid,
        in_specs=(
            P(AXES, None),
            P(AXES, None),
            P("r", FSDP, None),
            P("r", FSDP, None),
            P("r", FSDP, None),
            P("r", None, FSDP, None),
            P(None, FSDP, None),
            P(None, FSDP, None),
            P(),
        ),
        out_specs=(
            P("r", FSDP, None),
            P("r", FSDP, None),
            P("r", FSDP, None),
            P(FSDP, None),
            P(FSDP, None),
        ),
        check_vma=False,
    )
```

```python
import functools
import math

import jax
import jax.numpy as jnp
from jax import lax
from jax.experimental import pallas as pl
from jax.experimental.pallas import tpu as pltpu
from jax.sharding import Mesh
from jax.sharding import PartitionSpec as P

AXES = ("r", "z", "y", "x", "c")
FSDP = ("z", "y", "x", "c")
VMEM = pl.BlockSpec(memory_space=pltpu.VMEM)


def swap(block, axis, distance=1):
    size = lax.axis_size(axis)
    return lax.ppermute(block, axis, [(i, i ^ distance) for i in range(size)])


def pair_sum(block, axis, distance):
    groups = [[i, i ^ distance] for i in range(lax.axis_size(axis)) if not i & distance]
    both = lax.all_gather(block, axis, axis_index_groups=groups)
    return both[0] + both[1]


def exchange(blocks, axes):
    return lax.all_to_all(blocks, axes, split_axis=0, concat_axis=0, tiled=True)


def spread(block, axis):
    size = lax.axis_size(axis)
    return exchange(jnp.broadcast_to(block[None], (size, *block.shape)), axis)


def norm_kernel(sizes, act_ref, out_ref, chunk_ref, block_ref, in_sems, out_sems):
    nz, ny, nxc, rows = sizes
    tokens, features = act_ref.shape
    width, lanes, step = nxc * rows, 128, 256
    parts = range(nz * ny)
    arrive = [
        pltpu.make_async_copy(act_ref.at[:, pl.ds(i * width, width)], chunk_ref.at[i], in_sems.at[i])
        for i in parts
    ]
    leave = [
        pltpu.make_async_copy(block_ref.at[i], out_ref.at[:, i % ny, i // ny], out_sems.at[i])
        for i in parts
    ]
    for copy in arrive:
        copy.start()
    total = jnp.zeros((tokens, lanes), jnp.float32)
    for i in parts:
        arrive[i].wait()
        for k in range(0, width, lanes):
            part = chunk_ref[i, :, k : k + lanes].astype(jnp.float32)
            total = total + part * part
    total = jnp.sum(total, axis=1, keepdims=True)
    scale = lax.rsqrt(total * (1.0 / features) + 1e-05)
    scale = jnp.broadcast_to(scale, (tokens, lanes)).T[:1]
    one = (
        lax.broadcasted_iota(jnp.int32, (step, step), 0) == lax.broadcasted_iota(jnp.int32, (step, step), 1)
    ).astype(jnp.bfloat16)
    for i in parts:
        turned = [
            lax.dot_general(
                one,
                chunk_ref[i, :, k : k + step],
                (((1,), (1,)), ((), ())),
                preferred_element_type=jnp.float32,
            )
            for k in range(0, width, step)
        ]
        turned = (jnp.concatenate(turned, axis=0) * scale).astype(jnp.bfloat16)
        block_ref[i] = turned.reshape(nxc, rows, tokens)
        leave[i].start()
    for copy in leave:
        copy.wait()


def normed_blocks(activations, sizes):
    nz, ny, nxc, rows = sizes
    tokens = activations.shape[0]
    return pl.pallas_call(
        functools.partial(norm_kernel, sizes),
        out_shape=jax.ShapeDtypeStruct((nxc, ny, nz, rows, tokens), jnp.bfloat16),
        in_specs=[pl.BlockSpec(memory_space=pltpu.HBM)],
        out_specs=pl.BlockSpec(memory_space=pltpu.HBM),
        scratch_shapes=[
            pltpu.VMEM((nz * ny, tokens, nxc * rows), jnp.bfloat16),
            pltpu.VMEM((nz * ny, nxc, rows, tokens), jnp.bfloat16),
            pltpu.SemaphoreType.DMA((nz * ny,)),
            pltpu.SemaphoreType.DMA((nz * ny,)),
        ],
        compiler_params=pltpu.CompilerParams(vmem_limit_bytes=60 * 2**20),
        cost_estimate=pl.CostEstimate(
            flops=8 * activations.size, bytes_accessed=4 * activations.size, transcendentals=0
        ),
    )(activations)


def add_kernel(kept_ref, came_ref, out_ref, block_ref, sems):
    leave = [pltpu.make_async_copy(block_ref.at[i], out_ref.at[i], sems.at[i]) for i in range(out_ref.shape[0])]
    for i, copy in enumerate(leave):
        block_ref[i] = (kept_ref[i] + came_ref[i].astype(jnp.float32)).astype(block_ref.dtype)
        copy.start()
    for copy in leave:
        copy.wait()


def add_blocks(kept, came):
    return pl.pallas_call(
        add_kernel,
        out_shape=jax.ShapeDtypeStruct(came.shape, came.dtype),
        in_specs=[VMEM, VMEM],
        out_specs=pl.BlockSpec(memory_space=pltpu.HBM),
        scratch_shapes=[pltpu.VMEM(came.shape, came.dtype), pltpu.SemaphoreType.DMA((came.shape[0],))],
        compiler_params=pltpu.CompilerParams(vmem_limit_bytes=16 * 2**20),
        cost_estimate=pl.CostEstimate(flops=came.size, bytes_accessed=8 * came.size, transcendentals=0),
    )(kept, came)


def cotangent_kernel(factor, part_ref, target_ref, out_ref):
    total = part_ref[0].astype(jnp.float32)
    for i in range(1, part_ref.shape[0]):
        total = total + part_ref[i].astype(jnp.float32)
    block = ((total - target_ref[...].astype(jnp.float32)) * factor).astype(out_ref.dtype)
    for i in range(out_ref.shape[0]):
        out_ref[i] = block


def cotangents(factor, part, target):
    return pl.pallas_call(
        functools.partial(cotangent_kernel, factor),
        out_shape=jax.ShapeDtypeStruct(part.shape, target.dtype),
        in_specs=[VMEM, VMEM],
        out_specs=VMEM,
        compiler_params=pltpu.CompilerParams(vmem_limit_bytes=8 * 2**20),
        cost_estimate=pl.CostEstimate(flops=2 * part.size, bytes_accessed=5 * part.size, transcendentals=0),
    )(part, target)


def on_device(
    activations,
    targets,
    weights,
    first_moment,
    second_moment,
    local_frags,
    global_frags,
    momentum_frags,
    fragment_index,
):
    f32, bf16 = jnp.float32, jnp.bfloat16
    nz, ny, nx, nc = (lax.axis_size(a) for a in FSDP)
    z, c = lax.axis_index("z"), lax.axis_index("c")
    tokens, features = act_ref.shape
    width = nxc * rows
    parts = range(nz * ny)
    arrive = [
        pltpu.make_async_copy(act_ref.at[:, pl.ds(i * width, width)], chunk_ref.at[i], in_sems.at[i])
        for i in parts
    ]
    leave = [
        pltpu.make_async_copy(block_ref.at[i], out_ref.at[:, i % ny, i // ny], out_sems.at[i])
        for i in parts
    ]
    for copy in arrive:
        copy.start()
    total = jnp.zeros((tokens, 1), jnp.float32)
    for i in parts:
        arrive[i].wait()
        part = chunk_ref[i].astype(jnp.float32)
        total = total + jnp.sum(part * part, axis=1, keepdims=True)
    scale = lax.rsqrt(total * (1.0 / features) + 1e-05)
    for i in parts:
        part = (chunk_ref[i].astype(jnp.float32) * scale).astype(jnp.bfloat16)
        block_ref[i] = part.T.reshape(nxc, rows, tokens)
        leave[i].start()
    for copy in leave:
        copy.wait()


def normed_blocks(activations, sizes):
    nz, ny, nxc, rows = sizes
    tokens = activations.shape[0]
    return pl.pallas_call(
        functools.partial(norm_kernel, sizes),
        out_shape=jax.ShapeDtypeStruct((nxc, ny, nz, rows, tokens), jnp.bfloat16),
        in_specs=[pl.BlockSpec(memory_space=pltpu.HBM)],
        out_specs=pl.BlockSpec(memory_space=pltpu.HBM),
        scratch_shapes=[
            pltpu.VMEM((nz * ny, tokens, nxc * rows), jnp.bfloat16),
            pltpu.VMEM((nz * ny, nxc, rows, tokens), jnp.bfloat16),
            pltpu.SemaphoreType.DMA((nz * ny,)),
            pltpu.SemaphoreType.DMA((nz * ny,)),
        ],
        compiler_params=pltpu.CompilerParams(vmem_limit_bytes=60 * 2**20),
        cost_estimate=pl.CostEstimate(
            flops=8 * activations.size, bytes_accessed=4 * activations.size, transcendentals=0
        ),
    )(activations)


def on_device(
    activations,
    targets,
    weights,
    first_moment,
    second_moment,
    local_frags,
    global_frags,
    momentum_frags,
    fragment_index,
):
    f32, bf16 = jnp.float32, jnp.bfloat16
    nz, ny, nx, nc = (lax.axis_size(a) for a in FSDP)
    z, y, x, c = (lax.axis_index(a) for a in FSDP)
    tokens, features = activations.shape
    rows, columns = weights.shape[1:]
    group = ny * nz * rows

    chosen = fragment_index[0]
    local_part = lax.dynamic_index_in_dim(local_frags[0], chosen, 0, False)
    global_part = lax.dynamic_index_in_dim(global_frags, chosen, 0, False)
    moment_part = lax.dynamic_index_in_dim(momentum_frags, chosen, 0, False)
    delta = global_part - local_part

    master = weights[0]
    low = lax.all_gather(master.astype(bf16), "z")
    low = lax.all_gather(low, "y").reshape(group, columns)

    blocks = normed_blocks(activations, (nz, ny, nx * nc, rows))
    held = exchange(blocks.reshape(nx * nc, group, tokens), ("x", "c"))

    held = held.reshape(nx, nc, group, tokens)
    mine = lax.dynamic_index_in_dim(held, c, 1, False)
    theirs = lax.dynamic_index_in_dim(held, 1 - c, 1, False)

    send = jnp.einsum("sft,fn->stn", theirs, low, preferred_element_type=f32).astype(bf16)
    part = jnp.einsum("sft,fn->stn", mine, low, preferred_element_type=f32)
    part = add_blocks(part, swap(send, "c"))
    part, delta = lax.optimization_barrier((exchange(part, "x"), pair_sum(delta, "r", 1)))
    factor = 1.0 / math.sqrt(tokens * nz * ny * nx * nc)
    cotangent = cotangents(factor, part, targets)
    cotangent, delta = lax.optimization_barrier((cotangent, delta))
    near, delta = lax.optimization_barrier((exchange(cotangent, "x"), pair_sum(delta, "r", 2)))
    far = swap(near, "c")

    grad = jnp.einsum("sft,stn->fn", mine, near, preferred_element_type=f32)
    grad = grad + jnp.einsum("sft,stn->fn", theirs, far, preferred_element_type=f32)
    grad = grad.reshape(ny, nz, rows, columns).astype(bf16)
    delta, grad = lax.optimization_barrier((delta, grad))
    grad = exchange(grad, "y")
    mean_delta = pair_sum(delta, "r", 4) / lax.axis_size("r")
    new_momentum = 0.9 * moment_part + mean_delta
    new_global = global_part - 0.7 * (mean_delta + 0.9 * new_momentum)
    grad, new_global, new_momentum = lax.optimization_barrier((grad, new_global, new_momentum))
    sent = jnp.sum(lax.dynamic_index_in_dim(grad, 1 - z, 1, False).astype(f32), axis=0)
    came = lax.all_gather(sent.astype(bf16), "z")
    came, grad = lax.optimization_barrier((came, grad))
    kept = jnp.sum(lax.dynamic_index_in_dim(grad, z, 1, False).astype(f32), axis=0)
    gradient = kept + lax.dynamic_index_in_dim(came, 1 - z, 0, False).astype(f32)

    new_first = 0.9 * first_moment[0] + 0.1 * gradient
    new_second = 0.95 * second_moment[0] + 0.05 * gradient * gradient
    new_master = master - 0.01 * (new_first / (jnp.sqrt(new_second) + 1e-08) + 0.1 * master)

    return (new_master[None], new_first[None], new_second[None], new_global, new_momentum)


def solution(mesh):
    grid = Mesh(mesh.devices.reshape(mesh.shape["replica"], 2, 4, 4, 2), AXES)
    return jax.shard_map(
        on_device,
        mesh=grid,
        in_specs=(
            P(AXES, None),
            P(AXES, None),
            P("r", FSDP, None),
            P("r", FSDP, None),
            P("r", FSDP, None),
            P("r", None, FSDP, None),
            P(None, FSDP, None),
            P(None, FSDP, None),
            P(),
        ),
        out_specs=(
            P("r", FSDP, None),
            P("r", FSDP, None),
            P("r", FSDP, None),
            P(FSDP, None),
            P(FSDP, None),
        ),
        check_vma=False,
    )
```

```python
import functools
import math

import jax
import jax.numpy as jnp
from jax import lax
from jax.experimental import pallas as pl
from jax.experimental.pallas import tpu as pltpu
from jax.sharding import Mesh
from jax.sharding import PartitionSpec as P

AXES = ("r", "z", "y", "x", "c")
FSDP = ("z", "y", "x", "c")
VMEM = pl.BlockSpec(memory_space=pltpu.VMEM)


def swap(block, axis, distance=1):
    size = lax.axis_size(axis)
    return lax.ppermute(block, axis, [(i, i ^ distance) for i in range(size)])


def pair_sum(block, axis, distance):
    groups = [[i, i ^ distance] for i in range(lax.axis_size(axis)) if not i & distance]
    both = lax.all_gather(block, axis, axis_index_groups=groups)
    return both[0] + both[1]


def exchange(blocks, axes):
    return lax.all_to_all(blocks, axes, split_axis=0, concat_axis=0, tiled=True)


def spread(block, axis):
    size = lax.axis_size(axis)
    return exchange(jnp.broadcast_to(block[None], (size, *block.shape)), axis)


def norm_kernel(sizes, act_ref, out_ref, chunk_ref, block_ref, in_sems, out_sems):
    nz, ny, nxc, rows = sizes
    tokens, features = act_ref.shape
    width, lanes, step = nxc * rows, 128, 256
    parts = range(nz * ny)
    arrive = [
        pltpu.make_async_copy(act_ref.at[:, pl.ds(i * width, width)], chunk_ref.at[i], in_sems.at[i])
        for i in parts
    ]
    leave = [
        pltpu.make_async_copy(block_ref.at[i], out_ref.at[:, i % ny, i // ny], out_sems.at[i])
        for i in parts
    ]
    for copy in arrive:
        copy.start()
    total = jnp.zeros((tokens, lanes), jnp.float32)
    for i in parts:
        arrive[i].wait()
        for k in range(0, width, lanes):
            part = chunk_ref[i, :, k : k + lanes].astype(jnp.float32)
            total = total + part * part
    total = jnp.sum(total, axis=1, keepdims=True)
    scale = lax.rsqrt(total * (1.0 / features) + 1e-05)
    scale = jnp.broadcast_to(scale, (tokens, lanes)).T[:1]
    one = (
        lax.broadcasted_iota(jnp.int32, (step, step), 0) == lax.broadcasted_iota(jnp.int32, (step, step), 1)
    ).astype(jnp.bfloat16)
    for i in parts:
        turned = [
            lax.dot_general(
                one,
                chunk_ref[i, :, k : k + step],
                (((1,), (1,)), ((), ())),
                preferred_element_type=jnp.float32,
            )
            for k in range(0, width, step)
        ]
        turned = (jnp.concatenate(turned, axis=0) * scale).astype(jnp.bfloat16)
        block_ref[i] = turned.reshape(nxc, rows, tokens)
        leave[i].start()
    for copy in leave:
        copy.wait()


def normed_blocks(activations, sizes):
    nz, ny, nxc, rows = sizes
    tokens = activations.shape[0]
    return pl.pallas_call(
        functools.partial(norm_kernel, sizes),
        out_shape=jax.ShapeDtypeStruct((nxc, ny, nz, rows, tokens), jnp.bfloat16),
        in_specs=[pl.BlockSpec(memory_space=pltpu.HBM)],
        out_specs=pl.BlockSpec(memory_space=pltpu.HBM),
        scratch_shapes=[
            pltpu.VMEM((nz * ny, tokens, nxc * rows), jnp.bfloat16),
            pltpu.VMEM((nz * ny, nxc, rows, tokens), jnp.bfloat16),
            pltpu.SemaphoreType.DMA((nz * ny,)),
            pltpu.SemaphoreType.DMA((nz * ny,)),
        ],
        compiler_params=pltpu.CompilerParams(vmem_limit_bytes=60 * 2**20),
        cost_estimate=pl.CostEstimate(
            flops=8 * activations.size, bytes_accessed=4 * activations.size, transcendentals=0
        ),
    )(activations)


def add_kernel(kept_ref, came_ref, out_ref):
    out_ref[...] = (kept_ref[...] + came_ref[...].astype(jnp.float32)).astype(out_ref.dtype)


def add_blocks(kept, came):
    return pl.pallas_call(
        add_kernel,
        out_shape=jax.ShapeDtypeStruct(came.shape, came.dtype),
        in_specs=[VMEM, VMEM],
        out_specs=VMEM,
        compiler_params=pltpu.CompilerParams(vmem_limit_bytes=8 * 2**20),
        cost_estimate=pl.CostEstimate(flops=came.size, bytes_accessed=8 * came.size, transcendentals=0),
    )(kept, came)


def cotangent_kernel(factor, part_ref, target_ref, out_ref):
    total = part_ref[0].astype(jnp.float32)
    for i in range(1, part_ref.shape[0]):
        total = total + part_ref[i].astype(jnp.float32)
    block = ((total - target_ref[...].astype(jnp.float32)) * factor).astype(out_ref.dtype)
    for i in range(out_ref.shape[0]):
        out_ref[i] = block


def cotangents(factor, part, target):
    return pl.pallas_call(
        functools.partial(cotangent_kernel, factor),
        out_shape=jax.ShapeDtypeStruct(part.shape, target.dtype),
        in_specs=[VMEM, VMEM],
        out_specs=VMEM,
        compiler_params=pltpu.CompilerParams(vmem_limit_bytes=8 * 2**20),
        cost_estimate=pl.CostEstimate(flops=2 * part.size, bytes_accessed=5 * part.size, transcendentals=0),
    )(part, target)


def on_device(
    activations,
    targets,
    weights,
    first_moment,
    second_moment,
    local_frags,
    global_frags,
    momentum_frags,
    fragment_index,
):
    f32, bf16 = jnp.float32, jnp.bfloat16
    nz, ny, nx, nc = (lax.axis_size(a) for a in FSDP)
    z, c = lax.axis_index("z"), lax.axis_index("c")
    tokens, features = act_ref.shape
    width = nxc * rows
    parts = range(nz * ny)
    arrive = [
        pltpu.make_async_copy(act_ref.at[:, pl.ds(i * width, width)], chunk_ref.at[i], in_sems.at[i])
        for i in parts
    ]
    leave = [
        pltpu.make_async_copy(block_ref.at[i], out_ref.at[:, i % ny, i // ny], out_sems.at[i])
        for i in parts
    ]
    for copy in arrive:
        copy.start()
    total = jnp.zeros((tokens, 1), jnp.float32)
    for i in parts:
        arrive[i].wait()
        part = chunk_ref[i].astype(jnp.float32)
        total = total + jnp.sum(part * part, axis=1, keepdims=True)
    scale = lax.rsqrt(total * (1.0 / features) + 1e-05)
    for i in parts:
        part = (chunk_ref[i].astype(jnp.float32) * scale).astype(jnp.bfloat16)
        block_ref[i] = part.T.reshape(nxc, rows, tokens)
        leave[i].start()
    for copy in leave:
        copy.wait()


def normed_blocks(activations, sizes):
    nz, ny, nxc, rows = sizes
    tokens = activations.shape[0]
    return pl.pallas_call(
        functools.partial(norm_kernel, sizes),
        out_shape=jax.ShapeDtypeStruct((nxc, ny, nz, rows, tokens), jnp.bfloat16),
        in_specs=[pl.BlockSpec(memory_space=pltpu.HBM)],
        out_specs=pl.BlockSpec(memory_space=pltpu.HBM),
        scratch_shapes=[
            pltpu.VMEM((nz * ny, tokens, nxc * rows), jnp.bfloat16),
            pltpu.VMEM((nz * ny, nxc, rows, tokens), jnp.bfloat16),
            pltpu.SemaphoreType.DMA((nz * ny,)),
            pltpu.SemaphoreType.DMA((nz * ny,)),
        ],
        compiler_params=pltpu.CompilerParams(vmem_limit_bytes=60 * 2**20),
        cost_estimate=pl.CostEstimate(
            flops=8 * activations.size, bytes_accessed=4 * activations.size, transcendentals=0
        ),
    )(activations)


def on_device(
    activations,
    targets,
    weights,
    first_moment,
    second_moment,
    local_frags,
    global_frags,
    momentum_frags,
    fragment_index,
):
    f32, bf16 = jnp.float32, jnp.bfloat16
    nz, ny, nx, nc = (lax.axis_size(a) for a in FSDP)
    z, y, x, c = (lax.axis_index(a) for a in FSDP)
    tokens, features = activations.shape
    rows, columns = weights.shape[1:]
    group = ny * nz * rows

    chosen = fragment_index[0]
    local_part = lax.dynamic_index_in_dim(local_frags[0], chosen, 0, False)
    global_part = lax.dynamic_index_in_dim(global_frags, chosen, 0, False)
    moment_part = lax.dynamic_index_in_dim(momentum_frags, chosen, 0, False)
    delta = global_part - local_part

    master = weights[0]
    low = lax.all_gather(master.astype(bf16), "z")
    low = lax.all_gather(low, "y").reshape(group, columns)

    blocks = normed_blocks(activations, (nz, ny, nx * nc, rows))
    held = exchange(blocks.reshape(nx * nc, group, tokens), ("x", "c"))

    held = held.reshape(nx, nc, group, tokens)
    mine = lax.dynamic_index_in_dim(held, c, 1, False)
    theirs = lax.dynamic_index_in_dim(held, 1 - c, 1, False)

    send = jnp.einsum("sft,fn->stn", theirs, low, preferred_element_type=f32).astype(bf16)
    part = jnp.einsum("sft,fn->stn", mine, low, preferred_element_type=f32)
    part = add_blocks(part, swap(send, "c"))
    part, delta = lax.optimization_barrier((exchange(part, "x"), pair_sum(delta, "r", 1)))
    factor = 1.0 / math.sqrt(tokens * nz * ny * nx * nc)
    cotangent = cotangents(factor, part, targets)
    cotangent, delta = lax.optimization_barrier((cotangent, delta))
    near, delta = lax.optimization_barrier((exchange(cotangent, "x"), pair_sum(delta, "r", 2)))
    far = swap(near, "c")

    grad = jnp.einsum("sft,stn->fn", mine, near, preferred_element_type=f32)
    grad = grad + jnp.einsum("sft,stn->fn", theirs, far, preferred_element_type=f32)
    grad = grad.reshape(ny, nz, rows, columns).astype(bf16)
    delta, grad = lax.optimization_barrier((delta, grad))
    grad = exchange(grad, "y")
    mean_delta = pair_sum(delta, "r", 4) / lax.axis_size("r")
    new_momentum = 0.9 * moment_part + mean_delta
    new_global = global_part - 0.7 * (mean_delta + 0.9 * new_momentum)
    grad, new_global, new_momentum = lax.optimization_barrier((grad, new_global, new_momentum))
    grad = jnp.sum(grad.astype(f32), axis=0)
    sent = lax.dynamic_index_in_dim(grad, 1 - z, 0, False).astype(bf16)
    kept = lax.dynamic_index_in_dim(grad, z, 0, False)
    came = lax.dynamic_index_in_dim(lax.all_gather(sent, "z"), 1 - z, 0, False)
    gradient = kept + came.astype(f32)

    new_first = 0.9 * first_moment[0] + 0.1 * gradient
    new_second = 0.95 * second_moment[0] + 0.05 * gradient * gradient
    new_master = master - 0.01 * (new_first / (jnp.sqrt(new_second) + 1e-08) + 0.1 * master)

    return (new_master[None], new_first[None], new_second[None], new_global, new_momentum)


def solution(mesh):
    grid = Mesh(mesh.devices.reshape(mesh.shape["replica"], 2, 4, 4, 2), AXES)
    return jax.shard_map(
        on_device,
        mesh=grid,
        in_specs=(
            P(AXES, None),
            P(AXES, None),
            P("r", FSDP, None),
            P("r", FSDP, None),
            P("r", FSDP, None),
            P("r", None, FSDP, None),
            P(None, FSDP, None),
            P(None, FSDP, None),
            P(),
        ),
        out_specs=(
            P("r", FSDP, None),
            P("r", FSDP, None),
            P("r", FSDP, None),
            P(FSDP, None),
            P(FSDP, None),
        ),
        check_vma=False,
    )
```
